32 devices in a mesh: region: 2 (over x), space: 16 (over z, y, core).
Axes of the slice: x: 2, y: 2, z: 4, core: 2. Of those that a mesh axis runs over, the one named last changes fastest.
Arguments:
- right_side: float32 [8, 64, 8192], P('region', None, 'space'), parts along dimension 0, may hold values from -45 to 45
- obs_prec: float32 [128, 8192], P('region', 'space'), parts along dimension 0, may hold values from 0.2 to 5
- outlier_flags: int32 [128, 8192], P('region', 'space'), parts along dimension 0, may hold values 0 or 1
- up_one: float32 [64, 256, 128], P('space', 'region'), parts along dimension 1, may hold values from -0.015625 to 0.015625
- up_two: float32 [64, 256, 128], P('space', 'region'), parts along dimension 1, may hold values from -0.015625 to 0.015625
Outputs:
- smoothed: float32 [8, 64, 8192], P('region', None, 'space'), parts along dimension 0
- residual: float32 [8, 64, 8192], P('region', None, 'space'), parts along dimension 0
The draws below stay inside these ranges and needn't reach their ends.
There are 2 independent parts, one for each index of `region`. The reference program is written for one: setup_inputs(seed, part) draws one part's arguments, and reference() takes and returns one part's arrays. A program takes and returns all parts, laid end to end along the dimension named above; each array names one. Nothing has to cross between parts.
All inputs are finite; a program needn't handle non-finite values. No bound on the sum of `outlier_flags` on one device may be relied on, other than what follows from the above.
Results may differ from the reference program's by a relative error of at most 0.0003.
Values sent between devices are 32-bit elements; how exact they have to be, the bound alone decides.
A program may use at most 64 MiB of HBM per device.

```python
import math
import jax
import jax.numpy as jnp
from jax import lax

TILE = 128
DAYS = 64
FIELDS = 4
ITERS = 3
NC = 8192
NBLK = 64


def draw_right_side(key, part):
    key = jax.random.fold_in(key, 11)
    cell = jnp.arange(NC).astype(jnp.float32)
    scale = 2.0 * jnp.exp(math.log(3.0) * cell / (NC - 1))
    rough = jnp.clip(jax.random.normal(key, (FIELDS, DAYS, NC), jnp.float32), -4.0, 4.0)
    return (rough * scale).astype(jnp.float32)


def plant(values, stream_key, least, top_value):
    place = [jax.random.randint(jax.random.fold_in(stream_key, axis), (), 0, length) for axis, length in enumerate(values.shape)]
    main_axis = values.shape.index(max(values.shape))
    beside = place[:main_axis] + [(place[main_axis] + 1) % values.shape[main_axis]] + place[main_axis + 1:]
    return values.at[tuple(place)].set(least).at[tuple(beside)].set(top_value)


def levels(key, extent, pieces, smallest, high):
    def one(dim, parts):
        draws = jax.random.uniform(jax.random.fold_in(jax.random.fold_in(key, 6), dim), (parts,), jnp.float32, smallest / len(pieces), high / len(pieces))
        return jnp.repeat(jnp.exp(draws), extent[dim] // parts).reshape((-1,) + (1,) * (len(extent) - dim - 1))

    gain = one(*pieces[0])
    for cut in pieces[1:]:
        gain = gain * one(*cut)
    return gain


def setup_inputs(seed: int = 0, part: int = 0) -> dict:
    key_of = jax.random.split(jax.random.key(seed), 6)
    part_keys = jax.random.split(jax.random.fold_in(key_of[5], part), 6)
    return {
        "right_side": draw_right_side(jax.random.fold_in(jax.random.fold_in(key_of[5], part), 71), part),
        "obs_prec": jnp.clip(jnp.exp(math.log(5.0) - 3.218876 * jax.random.uniform(part_keys[1], (DAYS, NC), jnp.float32) ** levels(part_keys[1], (DAYS, NC), ((1, 16),), -0.2, 0.2)), 0.2, 5.0),
        "outlier_flags": plant((jax.random.randint(part_keys[2], (DAYS, NC), 0, 8) < 1).astype(jnp.int32), jax.random.fold_in(part_keys[2], 1), 0, 1),
        "up_one": jnp.clip(jax.random.uniform(part_keys[3], (NBLK, TILE, TILE), jnp.float32, -0.015625, 0.015625) * levels(part_keys[3], (NBLK, TILE, TILE), ((0, 16),), -0.4, 0.0), -0.015625, 0.015625),
        "up_two": jnp.clip(jax.random.uniform(part_keys[4], (NBLK, TILE, TILE), jnp.float32, -0.015625, 0.015625) * levels(part_keys[4], (NBLK, TILE, TILE), ((0, 16),), -0.4, 0.0), -0.015625, 0.015625),
    }


def spatial(field, up_one, up_two):
    nf, nd, ncell = field.shape
    nblk = ncell // TILE
    blocks = field.reshape(nf, nd, nblk, TILE)
    zeros_two = jnp.zeros((nf, nd, 2, TILE), jnp.float32)
    padded = jnp.concatenate([zeros_two, blocks, zeros_two], axis=2)
    output = 8.0 * blocks
    for reach, tiles in ((1, up_one), (2, up_two)):
        forward = jnp.einsum("fdbj,bij->fdbi", padded[:, :, 2 + reach:2 + reach + nblk], tiles, precision=lax.Precision.HIGHEST)
        backward = jnp.einsum("fdbi,bij->fdbj", blocks, tiles, precision=lax.Precision.HIGHEST)
        backward = jnp.concatenate([jnp.zeros((nf, nd, reach, TILE), jnp.float32), backward[:, :, :nblk - reach]], axis=2)
        output = output - forward - backward
    return output.reshape(nf, nd, ncell)


def lagged(field, lag):
    return jnp.concatenate([jnp.zeros_like(field[:, :lag]), field[:, :-lag]], axis=1)


def leading(field, lag):
    return jnp.concatenate([field[:, lag:], jnp.zeros_like(field[:, :lag])], axis=1)


def temporal(field):
    innov = field - 1.5 * lagged(field, 1) + 0.6 * lagged(field, 2)
    return innov - 1.5 * leading(innov, 1) + 0.6 * leading(innov, 2)


def reference(right_side, obs_prec, outlier_flags, up_one, up_two):
    weight = obs_prec * (1.0 - 0.9 * outlier_flags.astype(jnp.float32))

    def operate(field):
        return weight[None] * field + spatial(field, up_one, up_two) + 0.5 * temporal(field)

    smoothed = jnp.zeros_like(right_side)
    residual = right_side
    direction = right_side
    norm_now = jnp.sum(residual * residual, axis=(1, 2))[:, None, None]
    for step in range(ITERS):
        image = operate(direction)
        alpha = norm_now / jnp.sum(direction * image, axis=(1, 2))[:, None, None]
        smoothed = smoothed + alpha * direction
        residual = residual - alpha * image
        norm_next = jnp.sum(residual * residual, axis=(1, 2))[:, None, None]
        direction = residual + (norm_next / norm_now) * direction
        norm_now = norm_next
    return smoothed, residual
```

```python
import functools

import jax
import jax.numpy as jnp
from jax import lax
from jax.experimental import pallas as pl
from jax.experimental.pallas import tpu as pltpu
from jax.sharding import PartitionSpec as P

TILE = 128
ITERS = 3
GROUPS = 2
PAIR = 2 * TILE
F32 = jnp.float32
BF16 = jnp.bfloat16

FIRST_FIRST, SECOND_FIRST, FIRST_SECOND, SECOND_SECOND, RIGHT_SECOND, SECOND_NEXT = range(6)


def split(x):
    high = x.astype(BF16)
    return high, (x - high.astype(F32)).astype(BF16)


def temporal(x):
    days = x.shape[0]
    row = lax.broadcasted_iota(jnp.int32, x.shape, 0)

    def lagged(v, lag):
        return jnp.where(row >= lag, pltpu.roll(v, lag, 0), 0.0)

    def leading(v, lag):
        return jnp.where(row < days - lag, pltpu.roll(v, days - lag, 0), 0.0)

    innov = x - 1.5 * lagged(x, 1) + 0.6 * lagged(x, 2)
    return innov - 1.5 * leading(innov, 1) + 0.6 * leading(innov, 2)


def kernel(
    n, nf, days,
    rs, prec, flags, one, two,
    x, r,
    high, low, diag, p, w, cs, h_right, h_left, p_right, r_right, p_left, r_left, red,
    send_r, recv_r, send_l, recv_l, send_s, recv_s,
):
    me = lax.axis_index("space")
    per = nf // GROUPS
    rows = per * days
    half = (slice(0, PAIR), slice(PAIR, 2 * PAIR))

    barrier = pltpu.get_barrier_semaphore()

    def greet(step, carry):
        pl.semaphore_signal(
            barrier, inc=1, device_id={"space": lax.rem(me + step, n)},
            device_id_type=pl.DeviceIdType.MESH,
        )
        return carry

    lax.fori_loop(1, n, greet, 0)

    def put(place, a, b, value):
        hi, lo = split(value)
        at = (place, slice(a * TILE, (a + 1) * TILE), slice(b * TILE, (b + 1) * TILE))
        high[at] = hi
        low[at] = lo

    def dot(value, place):
        hi, lo = value
        return (
            jnp.dot(hi, high[place], preferred_element_type=F32)
            + jnp.dot(hi, low[place], preferred_element_type=F32)
            + jnp.dot(lo, high[place], preferred_element_type=F32)
        )

    def of_group(g):
        return slice(g * rows, (g + 1) * rows)

    def of_field(f):
        return slice(f * days, (f + 1) * days)

    def to_prev(e, g):
        src = rs.at[of_group(g), half[0]] if e == 0 else w.at[e - 1, 0, of_group(g)]
        return pltpu.make_async_remote_copy(
            src_ref=src, dst_ref=h_right.at[e, of_group(g)],
            send_sem=send_r.at[e, g], recv_sem=recv_r.at[e, g],
            device_id={"space": jnp.maximum(me - 1, 0)},
            device_id_type=pl.DeviceIdType.MESH,
        )

    def to_next(e, g):
        return pltpu.make_async_remote_copy(
            src_ref=cs.at[e, of_group(g)], dst_ref=h_left.at[e, of_group(g)],
            send_sem=send_l.at[e, g], recv_sem=recv_l.at[e, g],
            device_id={"space": jnp.minimum(me + 1, n - 1)},
            device_id_type=pl.DeviceIdType.MESH,
        )

    zero = jnp.zeros((TILE, TILE), F32)
    put(SECOND_NEXT, 0, 0, two[2])
    put(SECOND_NEXT, 0, 1, zero)
    put(SECOND_NEXT, 1, 0, one[3])
    put(SECOND_NEXT, 1, 1, two[3])
    pl.semaphore_wait(barrier, n - 1)

    for g in range(GROUPS):
        @pl.when(me > 0)
        def _():
            to_prev(0, g).start()

        cs[0, of_group(g)] = dot(split(rs[of_group(g), half[1]]), SECOND_NEXT)

        @pl.when(me < n - 1)
        def _():
            to_next(0, g).start()

    @pl.when(me == 0)
    def _():
        h_left[...] = jnp.zeros_like(h_left)

    @pl.when(me == n - 1)
    def _():
        h_right[...] = jnp.zeros_like(h_right)

    for place, at in ((FIRST_FIRST, 0), (SECOND_SECOND, 2)):
        put(place, 0, 0, zero)
        put(place, 0, 1, one[at])
        put(place, 1, 0, one[at].T)
        put(place, 1, 1, zero)
    put(FIRST_SECOND, 0, 0, two[0])
    put(FIRST_SECOND, 0, 1, zero)
    put(FIRST_SECOND, 1, 0, one[1])
    put(FIRST_SECOND, 1, 1, two[1])
    for place, at in ((SECOND_FIRST, 0), (RIGHT_SECOND, 2)):
        put(place, 0, 0, two[at].T)
        put(place, 0, 1, one[at + 1].T)
        put(place, 1, 0, zero)
        put(place, 1, 1, two[at + 1].T)
    diag[...] = 8.0 + prec[...] * (1.0 - 0.9 * flags[...].astype(F32))

    def sums_wait(j):
        every = red.at[j, pl.ds(0, n - 1)]
        return pltpu.make_async_copy(every, every, recv_s.at[j])

    def sums_sent(j):
        every = red.at[j, pl.ds(0, n - 1)]
        return pltpu.make_async_copy(every, every, send_s.at[j])

    def send_sums(j, parts):
        kinds = len(parts[0])
        flat = [s for field in parts for s in field]
        column = jnp.concatenate([jnp.sum(s, axis=0, keepdims=True) for s in flat], axis=0)
        column = jnp.sum(column, axis=1, keepdims=True)
        shape = (len(flat), TILE)
        keep = lax.broadcasted_iota(jnp.int32, shape, 0) == lax.broadcasted_iota(jnp.int32, shape, 1)
        red[j, me] = jnp.sum(jnp.where(keep, column, 0.0), axis=0, keepdims=True)

        def send(step, carry):
            pltpu.make_async_remote_copy(
                src_ref=red.at[j, me], dst_ref=red.at[j, me],
                send_sem=send_s.at[j], recv_sem=recv_s.at[j],
                device_id={"space": lax.rem(me + step, n)},
                device_id_type=pl.DeviceIdType.MESH,
            ).start()
            return carry

        lax.fori_loop(1, n, send, 0)

    def totals(j, kinds):
        sums_wait(j).wait()
        total = jnp.sum(red[j], axis=0)
        shape = (8, TILE)
        row = lax.broadcasted_iota(jnp.int32, shape, 0)
        lane = lax.broadcasted_iota(jnp.int32, shape, 1)
        total = jnp.broadcast_to(total, shape)
        return [
            jnp.sum(jnp.where(lane == kinds * row + kind, total, 0.0), axis=1, keepdims=True)
            for kind in range(kinds)
        ]

    def fold(a):
        return jnp.sum(a.reshape(days // 8, 8, a.shape[1]), axis=0)

    def folded(a, b):
        s = fold(a * b)
        return s[:, :TILE] + s[:, TILE:]

    for k in range(ITERS):
        last = k == ITERS - 1
        for g in range(GROUPS):
            group = of_group(g)
            j = k * GROUPS + g
            if k == 0:
                p[0, group] = rs[group, half[0]]
                p[1, group] = rs[group, half[1]]
                r[group] = rs[group]
                x[group] = jnp.zeros_like(x[group])
            else:
                rr, pw, rw, ww = totals(j - GROUPS, 4)
                alpha = rr / pw
                beta = (rr + alpha * (alpha * ww - 2.0 * rw)) / rr
                for i in range(per):
                    field = of_field(g * per + i)
                    a, b = alpha[i : i + 1], beta[i : i + 1]
                    for s in range(2):
                        x[field, half[s]] += a * p[s, field]
                        res = r[field, half[s]] - a * w[k - 1, s, field]
                        r[field, half[s]] = res
                        p[s, field] = res + b * p[s, field]
            first, second = split(p[0, group]), split(p[1, group])
            near = dot(first, FIRST_FIRST) + dot(second, SECOND_FIRST)
            far = dot(first, FIRST_SECOND) + dot(second, SECOND_SECOND)
            for i in range(per):
                field = of_field(g * per + i)
                for s, coupled in ((0, near), (1, far)):
                    v = p[s, field]
                    w[k, s, field] = (
                        diag[:, half[s]] * v + 0.5 * temporal(v)
                        - coupled[i * days : (i + 1) * days]
                    )

            @pl.when(me > 0)
            def _():
                to_next(k, g).wait_recv()

            @pl.when(me < n - 1)
            def _():
                to_prev(k, g).wait_recv()

            if k == 0:
                for dst in (p_right, r_right):
                    dst[group] = h_right[k, group]
                for dst in (p_left, r_left):
                    dst[group] = h_left[k, group]
            else:
                for i in range(per):
                    field = of_field(g * per + i)
                    a, b = alpha[i : i + 1], beta[i : i + 1]
                    for pp, res, new in ((p_left, r_left, h_left), (p_right, r_right, h_right)):
                        value = res[field] - a * new[k, field]
                        res[field] = value
                        pp[field] = value + b * pp[field]
            w[k, 0, group] -= p_left[group]
            if not last:
                @pl.when(me > 0)
                def _():
                    to_prev(k + 1, g).start()
            w[k, 1, group] -= dot(split(p_right[group]), RIGHT_SECOND)
            if not last:
                cs[k + 1, group] = dot(split(w[k, 1, group]), SECOND_NEXT)

                @pl.when(me < n - 1)
                def _():
                    to_next(k + 1, g).start()

            parts = []
            for i in range(per):
                field = of_field(g * per + i)
                sums = [0.0] * (2 if last else 4)
                for s in range(2):
                    image, res = w[k, s, field], r[field, half[s]]
                    sums[0] += folded(res, res)
                    sums[1] += folded(p[s, field], image)
                    if not last:
                        sums[2] += folded(res, image)
                        sums[3] += folded(image, image)
                parts.append(sums)
            send_sums(j, parts)

    for g in range(GROUPS):
        rr, pw = totals((ITERS - 1) * GROUPS + g, 2)
        alpha = rr / pw
        for i in range(per):
            field = of_field(g * per + i)
            a = alpha[i : i + 1]
            for s in range(2):
                x[field, half[s]] += a * p[s, field]
                r[field, half[s]] -= a * w[ITERS - 1, s, field]

    for k in range(ITERS):
        for g in range(GROUPS):
            @pl.when(me > 0)
            def _():
                to_prev(k, g).wait_send()

            @pl.when(me < n - 1)
            def _():
                to_next(k, g).wait_send()

            sums_sent(k * GROUPS + g).wait()


def on_device(n, right_side, obs_prec, outlier_flags, up_one, up_two):
    nf, days, cells = right_side.shape
    rows = nf * days
    vmem = pl.BlockSpec(memory_space=pltpu.VMEM)
    side = pltpu.VMEM((rows, PAIR), F32)
    sides = pltpu.VMEM((ITERS, rows, PAIR), F32)
    dma = pltpu.SemaphoreType.DMA
    smoothed, residual = pl.pallas_call(
        functools.partial(kernel, n, nf, days),
        out_shape=[jax.ShapeDtypeStruct((rows, cells), F32)] * 2,
        in_specs=[vmem] * 5,
        out_specs=[vmem] * 2,
        scratch_shapes=[
            pltpu.VMEM((6, PAIR, PAIR), BF16),
            pltpu.VMEM((6, PAIR, PAIR), BF16),
            pltpu.VMEM((days, cells), F32),
            pltpu.VMEM((2, rows, PAIR), F32),
            pltpu.VMEM((ITERS, 2, rows, PAIR), F32),
            sides, sides, sides,
            side, side, side, side,
            pltpu.VMEM((ITERS * GROUPS, n, 1, TILE), F32),
            dma((ITERS, GROUPS)), dma((ITERS, GROUPS)),
            dma((ITERS, GROUPS)), dma((ITERS, GROUPS)),
            dma((ITERS * GROUPS,)), dma((ITERS * GROUPS,)),
        ],
        compiler_params=pltpu.CompilerParams(
            collective_id=0, has_side_effects=True, vmem_limit_bytes=40 * 2**20
        ),
        cost_estimate=pl.CostEstimate(
            flops=36 * ITERS * rows * PAIR * PAIR, bytes_accessed=12 * rows * cells, transcendentals=0
        ),
    )(right_side.reshape(rows, cells), obs_prec, outlier_flags, up_one, up_two)
    shape = (nf, days, cells)
    return smoothed.reshape(shape), residual.reshape(shape)


def solution(mesh):
    placed = (
        P("region", None, "space"),
        P("region", "space"),
        P("region", "space"),
        P("space", "region", None),
        P("space", "region", None),
    )
    return jax.shard_map(
        functools.partial(on_device, mesh.shape["space"]),
        mesh=mesh,
        in_specs=placed,
        out_specs=(P("region", None, "space"), P("region", None, "space")),
        check_vma=False,
    )
```

```python
import functools

import jax
import jax.numpy as jnp
from jax import lax
from jax.experimental import pallas as pl
from jax.experimental.pallas import tpu as pltpu
from jax.sharding import PartitionSpec as P

TILE = 128
ITERS = 3
GROUPS = 4
PAIR = 2 * TILE
F32 = jnp.float32
BF16 = jnp.bfloat16

FIRST_FIRST, SECOND_FIRST, FIRST_SECOND, SECOND_SECOND, RIGHT_SECOND, SECOND_NEXT = range(6)


def split(x):
    high = x.astype(BF16)
    return high, (x - high.astype(F32)).astype(BF16)


def temporal(x):
    days = x.shape[0]
    row = lax.broadcasted_iota(jnp.int32, x.shape, 0)

    def lagged(v, lag):
        return jnp.where(row >= lag, pltpu.roll(v, lag, 0), 0.0)

    def leading(v, lag):
        return jnp.where(row < days - lag, pltpu.roll(v, days - lag, 0), 0.0)

    innov = x - 1.5 * lagged(x, 1) + 0.6 * lagged(x, 2)
    return innov - 1.5 * leading(innov, 1) + 0.6 * leading(innov, 2)


def kernel(
    n, nf, days,
    rs_hbm, prec_hbm, flags_hbm, one_hbm, two_hbm,
    x, r,
    rs, prec, flags, one, two,
    high, low, diag, p, w, cs, h_right, h_left, p_right, r_right, p_left, r_left, red,
    send_r, recv_r, send_l, recv_l, send_s, recv_s, load,
):
    me = lax.axis_index("space")
    per = nf // GROUPS
    rows = per * days
    half = (slice(0, PAIR), slice(PAIR, 2 * PAIR))

    loads = [
        pltpu.make_async_copy(src, dst, load.at[i])
        for i, (src, dst) in enumerate(
            ((two_hbm, two), (one_hbm, one), (rs_hbm, rs), (prec_hbm, prec), (flags_hbm, flags))
        )
    ]
    for copy in loads:
        copy.start()

    barrier = pltpu.get_barrier_semaphore()

    def greet(step, carry):
        pl.semaphore_signal(
            barrier, inc=1, device_id={"space": lax.rem(me + step, n)},
            device_id_type=pl.DeviceIdType.MESH,
        )
        return carry

    lax.fori_loop(1, n, greet, 0)

    def put(place, a, b, value):
        hi, lo = split(value)
        at = (place, slice(a * TILE, (a + 1) * TILE), slice(b * TILE, (b + 1) * TILE))
        high[at] = hi
        low[at] = lo

    def dot(value, place):
        hi, lo = value
        return (
            jnp.dot(hi, high[place], preferred_element_type=F32)
            + jnp.dot(hi, low[place], preferred_element_type=F32)
            + jnp.dot(lo, high[place], preferred_element_type=F32)
        )

    def of_group(g):
        return slice(g * rows, (g + 1) * rows)

    def of_field(f):
        return slice(f * days, (f + 1) * days)

    def to_prev(e, g):
        src = rs.at[of_group(g), half[0]] if e == 0 else w.at[e - 1, 0, of_group(g)]
        return pltpu.make_async_remote_copy(
            src_ref=src, dst_ref=h_right.at[e, of_group(g)],
            send_sem=send_r.at[e, g], recv_sem=recv_r.at[e, g],
            device_id={"space": jnp.maximum(me - 1, 0)},
            device_id_type=pl.DeviceIdType.MESH,
        )

    def to_next(e, g):
        return pltpu.make_async_remote_copy(
            src_ref=cs.at[e, of_group(g)], dst_ref=h_left.at[e, of_group(g)],
            send_sem=send_l.at[e, g], recv_sem=recv_l.at[e, g],
            device_id={"space": jnp.minimum(me + 1, n - 1)},
            device_id_type=pl.DeviceIdType.MESH,
        )

    zero = jnp.zeros((TILE, TILE), F32)
    for copy in loads:
        copy.wait()
    put(SECOND_NEXT, 0, 0, two[2])
    put(SECOND_NEXT, 0, 1, zero)
    put(SECOND_NEXT, 1, 0, one[3])
    put(SECOND_NEXT, 1, 1, two[3])
    pl.semaphore_wait(barrier, n - 1)

    for g in range(GROUPS):
        @pl.when(me > 0)
        def _():
            to_prev(0, g).start()

        cs[0, of_group(g)] = dot(split(rs[of_group(g), half[1]]), SECOND_NEXT)

        @pl.when(me < n - 1)
        def _():
            to_next(0, g).start()

    @pl.when(me == 0)
    def _():
        h_left[...] = jnp.zeros_like(h_left)

    @pl.when(me == n - 1)
    def _():
        h_right[...] = jnp.zeros_like(h_right)

    for place, at in ((FIRST_FIRST, 0), (SECOND_SECOND, 2)):
        put(place, 0, 0, zero)
        put(place, 0, 1, one[at])
        put(place, 1, 0, one[at].T)
        put(place, 1, 1, zero)
    put(FIRST_SECOND, 0, 0, two[0])
    put(FIRST_SECOND, 0, 1, zero)
    put(FIRST_SECOND, 1, 0, one[1])
    put(FIRST_SECOND, 1, 1, two[1])
    for place, at in ((SECOND_FIRST, 0), (RIGHT_SECOND, 2)):
        put(place, 0, 0, two[at].T)
        put(place, 0, 1, one[at + 1].T)
        put(place, 1, 0, zero)
        put(place, 1, 1, two[at + 1].T)
    diag[...] = 8.0 + prec[...] * (1.0 - 0.9 * flags[...].astype(F32))

    def sums_wait(j):
        every = red.at[j, pl.ds(0, n - 1)]
        return pltpu.make_async_copy(every, every, recv_s.at[j])

    def sums_sent(j):
        every = red.at[j, pl.ds(0, n - 1)]
        return pltpu.make_async_copy(every, every, send_s.at[j])

    def send_sums(j, parts):
        flat = [s for field in parts for s in field]
        column = jnp.concatenate([jnp.sum(s, axis=0, keepdims=True) for s in flat], axis=0)
        column = jnp.sum(column, axis=1, keepdims=True)
        shape = (len(flat), TILE)
        keep = lax.broadcasted_iota(jnp.int32, shape, 0) == lax.broadcasted_iota(jnp.int32, shape, 1)
        red[j, me] = jnp.sum(jnp.where(keep, column, 0.0), axis=0, keepdims=True)

        def send(step, carry):
            pltpu.make_async_remote_copy(
                src_ref=red.at[j, me], dst_ref=red.at[j, me],
                send_sem=send_s.at[j], recv_sem=recv_s.at[j],
                device_id={"space": lax.rem(me + step, n)},
                device_id_type=pl.DeviceIdType.MESH,
            ).start()
            return carry

        lax.fori_loop(1, n, send, 0)

    def totals(j, kinds):
        sums_wait(j).wait()
        total = jnp.sum(red[j], axis=0)
        shape = (8, TILE)
        row = lax.broadcasted_iota(jnp.int32, shape, 0)
        lane = lax.broadcasted_iota(jnp.int32, shape, 1)
        total = jnp.broadcast_to(total, shape)
        return [
            jnp.sum(jnp.where(lane == kinds * row + kind, total, 0.0), axis=1, keepdims=True)
            for kind in range(kinds)
        ]

    def fold(a):
        return jnp.sum(a.reshape(days // 8, 8, a.shape[1]), axis=0)

    def folded(a, b):
        s = fold(a * b)
        return s[:, :TILE] + s[:, TILE:]

    def direction(k, s, at):
        return rs[at, half[s]] if k == 0 else p[s, at]

    def residue(k, s, at):
        return (rs if k == 0 else r)[at, half[s]]

    for k in range(ITERS):
        last = k == ITERS - 1
        for g in range(GROUPS):
            group = of_group(g)
            j = k * GROUPS + g
            if k > 0:
                rr, pw, rw, ww = totals(j - GROUPS, 4)
                alpha = rr / pw
                beta = (rr + alpha * (alpha * ww - 2.0 * rw)) / rr
                for i in range(per):
                    field = of_field(g * per + i)
                    a, b = alpha[i : i + 1], beta[i : i + 1]
                    for s in range(2):
                        old = direction(k - 1, s, field)
                        if k == 1:
                            x[field, half[s]] = a * old
                        else:
                            x[field, half[s]] += a * old
                        res = residue(k - 1, s, field) - a * w[k - 1, s, field]
                        r[field, half[s]] = res
                        p[s, field] = res + b * old
            first, second = (split(direction(k, s, group)) for s in range(2))
            near = dot(first, FIRST_FIRST) + dot(second, SECOND_FIRST)
            far = dot(first, FIRST_SECOND) + dot(second, SECOND_SECOND)
            for i in range(per):
                field = of_field(g * per + i)
                for s, coupled in ((0, near), (1, far)):
                    v = direction(k, s, field)
                    w[k, s, field] = (
                        diag[:, half[s]] * v + 0.5 * temporal(v)
                        - coupled[i * days : (i + 1) * days]
                    )

            @pl.when(me > 0)
            def _():
                to_next(k, g).wait_recv()

            @pl.when(me < n - 1)
            def _():
                to_prev(k, g).wait_recv()

            if k == 0:
                for dst in (p_right, r_right):
                    dst[group] = h_right[k, group]
                for dst in (p_left, r_left):
                    dst[group] = h_left[k, group]
            else:
                for i in range(per):
                    field = of_field(g * per + i)
                    a, b = alpha[i : i + 1], beta[i : i + 1]
                    for pp, res, new in ((p_left, r_left, h_left), (p_right, r_right, h_right)):
                        value = res[field] - a * new[k, field]
                        res[field] = value
                        pp[field] = value + b * pp[field]
            w[k, 0, group] -= p_left[group]
            w[k, 1, group] -= dot(split(p_right[group]), RIGHT_SECOND)
            if not last:
                cs[k + 1, group] = dot(split(w[k, 1, group]), SECOND_NEXT)

            parts = []
            for i in range(per):
                field = of_field(g * per + i)
                sums = [0.0] * (2 if last else 4)
                for s in range(2):
                    image, res = w[k, s, field], residue(k, s, field)
                    sums[0] += folded(res, res)
                    sums[1] += folded(direction(k, s, field), image)
                    if not last:
                        sums[2] += folded(res, image)
                        sums[3] += folded(image, image)
                parts.append(sums)
            send_sums(j, parts)
            if not last:
                @pl.when(me > 0)
                def _():
                    to_prev(k + 1, g).start()

                @pl.when(me < n - 1)
                def _():
                    to_next(k + 1, g).start()

    for g in range(GROUPS):
        rr, pw = totals((ITERS - 1) * GROUPS + g, 2)
        alpha = rr / pw
        for i in range(per):
            field = of_field(g * per + i)
            a = alpha[i : i + 1]
            for s in range(2):
                x[field, half[s]] += a * p[s, field]
                r[field, half[s]] -= a * w[ITERS - 1, s, field]

    for k in range(ITERS):
        for g in range(GROUPS):
            @pl.when(me > 0)
            def _():
                to_prev(k, g).wait_send()

            @pl.when(me < n - 1)
            def _():
                to_next(k, g).wait_send()

            sums_sent(k * GROUPS + g).wait()


def on_device(n, right_side, obs_prec, outlier_flags, up_one, up_two):
    nf, days, cells = right_side.shape
    rows = nf * days
    vmem = pl.BlockSpec(memory_space=pltpu.VMEM)
    side = pltpu.VMEM((rows, PAIR), F32)
    sides = pltpu.VMEM((ITERS, rows, PAIR), F32)
    dma = pltpu.SemaphoreType.DMA
    smoothed, residual = pl.pallas_call(
        functools.partial(kernel, n, nf, days),
        out_shape=[jax.ShapeDtypeStruct((rows, cells), F32)] * 2,
        in_specs=[pl.BlockSpec(memory_space=pltpu.HBM)] * 5,
        out_specs=[vmem] * 2,
        scratch_shapes=[
            pltpu.VMEM((rows, cells), F32),
            pltpu.VMEM(obs_prec.shape, F32),
            pltpu.VMEM(outlier_flags.shape, jnp.int32),
            pltpu.VMEM(up_one.shape, F32),
            pltpu.VMEM(up_two.shape, F32),
            pltpu.VMEM((6, PAIR, PAIR), BF16),
            pltpu.VMEM((6, PAIR, PAIR), BF16),
            pltpu.VMEM((days, cells), F32),
            pltpu.VMEM((2, rows, PAIR), F32),
            pltpu.VMEM((ITERS, 2, rows, PAIR), F32),
            sides, sides, sides,
            side, side, side, side,
            pltpu.VMEM((ITERS * GROUPS, n, 1, TILE), F32),
            dma((ITERS, GROUPS)), dma((ITERS, GROUPS)),
            dma((ITERS, GROUPS)), dma((ITERS, GROUPS)),
            dma((ITERS * GROUPS,)), dma((ITERS * GROUPS,)), dma((5,)),
        ],
        compiler_params=pltpu.CompilerParams(
            collective_id=0, has_side_effects=True, vmem_limit_bytes=63 * 2**20
        ),
        cost_estimate=pl.CostEstimate(
            flops=36 * ITERS * rows * PAIR * PAIR, bytes_accessed=12 * rows * cells, transcendentals=0
        ),
    )(right_side.reshape(rows, cells), obs_prec, outlier_flags, up_one, up_two)
    shape = (nf, days, cells)
    return smoothed.reshape(shape), residual.reshape(shape)


def solution(mesh):
    placed = (
        P("region", None, "space"),
        P("region", "space"),
        P("region", "space"),
        P("space", "region", None),
        P("space", "region", None),
    )
    return jax.shard_map(
        functools.partial(on_device, mesh.shape["space"]),
        mesh=mesh,
        in_specs=placed,
        out_specs=(P("region", None, "space"), P("region", None, "space")),
        check_vma=False,
    )
```

```python
import functools

import jax
import jax.numpy as jnp
from jax import lax
from jax.experimental import pallas as pl
from jax.experimental.pallas import tpu as pltpu
from jax.sharding import PartitionSpec as P

TILE = 128
ITERS = 3
GROUPS = 4
PAIR = 2 * TILE
F32 = jnp.float32
BF16 = jnp.bfloat16

FIRST_FIRST, SECOND_FIRST, FIRST_SECOND, SECOND_SECOND, RIGHT_SECOND, SECOND_NEXT = range(6)


def split(x):
    high = x.astype(BF16)
    return high, (x - high.astype(F32)).astype(BF16)


def temporal(x):
    days = x.shape[0]
    row = lax.broadcasted_iota(jnp.int32, x.shape, 0)

    def lagged(v, lag):
        return jnp.where(row >= lag, pltpu.roll(v, lag, 0), 0.0)

    def leading(v, lag):
        return jnp.where(row < days - lag, pltpu.roll(v, days - lag, 0), 0.0)

    innov = x - 1.5 * lagged(x, 1) + 0.6 * lagged(x, 2)
    return innov - 1.5 * leading(innov, 1) + 0.6 * leading(innov, 2)


def kernel(
    n, nf, days,
    rs_hbm, prec_hbm, flags_hbm, one_hbm, two_hbm,
    x, r,
    rs, prec, flags, one, two,
    high, low, diag, p, w, cs, h_right, h_left, p_right, r_right, p_left, r_left, red,
    send_r, recv_r, send_l, recv_l, send_s, recv_s, load,
):
    me = lax.axis_index("space")
    per = nf // GROUPS
    rows = per * days
    half = (slice(0, PAIR), slice(PAIR, 2 * PAIR))

    loads = [
        pltpu.make_async_copy(src, dst, load.at[i])
        for i, (src, dst) in enumerate(
            ((two_hbm, two), (one_hbm, one), (rs_hbm, rs), (prec_hbm, prec), (flags_hbm, flags))
        )
    ]
    for copy in loads:
        copy.start()

    barrier = pltpu.get_barrier_semaphore()

    def greet(step, carry):
        pl.semaphore_signal(
            barrier, inc=1, device_id={"space": lax.rem(me + step, n)},
            device_id_type=pl.DeviceIdType.MESH,
        )
        return carry

    lax.fori_loop(1, n, greet, 0)

    def put(place, a, b, value):
        hi, lo = split(value)
        at = (place, slice(a * TILE, (a + 1) * TILE), slice(b * TILE, (b + 1) * TILE))
        high[at] = hi
        low[at] = lo

    def dot(value, place):
        hi, lo = value
        return (
            jnp.dot(hi, high[place], preferred_element_type=F32)
            + jnp.dot(hi, low[place], preferred_element_type=F32)
            + jnp.dot(lo, high[place], preferred_element_type=F32)
        )

    def of_group(g):
        return slice(g * rows, (g + 1) * rows)

    def of_field(f):
        return slice(f * days, (f + 1) * days)

    def to_prev(e, g):
        src = rs_hbm.at[of_group(g), half[0]] if e == 0 else w.at[e - 1, 0, of_group(g)]
        return pltpu.make_async_remote_copy(
            src_ref=src, dst_ref=h_right.at[e, of_group(g)],
            send_sem=send_r.at[e, g], recv_sem=recv_r.at[e, g],
            device_id={"space": jnp.maximum(me - 1, 0)},
            device_id_type=pl.DeviceIdType.MESH,
        )

    def to_next(e, g):
        return pltpu.make_async_remote_copy(
            src_ref=cs.at[e, of_group(g)], dst_ref=h_left.at[e, of_group(g)],
            send_sem=send_l.at[e, g], recv_sem=recv_l.at[e, g],
            device_id={"space": jnp.minimum(me + 1, n - 1)},
            device_id_type=pl.DeviceIdType.MESH,
        )

    zero = jnp.zeros((TILE, TILE), F32)
    for copy in loads:
        copy.wait()
    put(SECOND_NEXT, 0, 0, two[2])
    put(SECOND_NEXT, 0, 1, zero)
    put(SECOND_NEXT, 1, 0, one[3])
    put(SECOND_NEXT, 1, 1, two[3])
    pl.semaphore_wait(barrier, n - 1)

    for g in range(GROUPS):
        @pl.when(me > 0)
        def _():
            to_prev(0, g).start()

        cs[0, of_group(g)] = dot(split(rs[of_group(g), half[1]]), SECOND_NEXT)

        @pl.when(me < n - 1)
        def _():
            to_next(0, g).start()

    @pl.when(me == 0)
    def _():
        h_left[...] = jnp.zeros_like(h_left)

    @pl.when(me == n - 1)
    def _():
        h_right[...] = jnp.zeros_like(h_right)

    for place, at in ((FIRST_FIRST, 0), (SECOND_SECOND, 2)):
        put(place, 0, 0, zero)
        put(place, 0, 1, one[at])
        put(place, 1, 0, one[at].T)
        put(place, 1, 1, zero)
    put(FIRST_SECOND, 0, 0, two[0])
    put(FIRST_SECOND, 0, 1, zero)
    put(FIRST_SECOND, 1, 0, one[1])
    put(FIRST_SECOND, 1, 1, two[1])
    for place, at in ((SECOND_FIRST, 0), (RIGHT_SECOND, 2)):
        put(place, 0, 0, two[at].T)
        put(place, 0, 1, one[at + 1].T)
        put(place, 1, 0, zero)
        put(place, 1, 1, two[at + 1].T)
    diag[...] = 8.0 + prec[...] * (1.0 - 0.9 * flags[...].astype(F32))

    def sums_wait(j):
        every = red.at[j, pl.ds(0, n - 1)]
        return pltpu.make_async_copy(every, every, recv_s.at[j])

    def sums_sent(j):
        every = red.at[j, pl.ds(0, n - 1)]
        return pltpu.make_async_copy(every, every, send_s.at[j])

    def send_sums(j, parts):
        flat = [s for field in parts for s in field]
        column = jnp.concatenate([jnp.sum(s, axis=0, keepdims=True) for s in flat], axis=0)
        column = jnp.sum(column, axis=1, keepdims=True)
        shape = (len(flat), TILE)
        keep = lax.broadcasted_iota(jnp.int32, shape, 0) == lax.broadcasted_iota(jnp.int32, shape, 1)
        red[j, me] = jnp.sum(jnp.where(keep, column, 0.0), axis=0, keepdims=True)

        def send(step, carry):
            pltpu.make_async_remote_copy(
                src_ref=red.at[j, me], dst_ref=red.at[j, me],
                send_sem=send_s.at[j], recv_sem=recv_s.at[j],
                device_id={"space": lax.rem(me + step, n)},
                device_id_type=pl.DeviceIdType.MESH,
            ).start()
            return carry

        lax.fori_loop(1, n, send, 0)

    def totals(j, kinds):
        sums_wait(j).wait()
        total = jnp.sum(red[j], axis=0)
        shape = (8, TILE)
        row = lax.broadcasted_iota(jnp.int32, shape, 0)
        lane = lax.broadcasted_iota(jnp.int32, shape, 1)
        total = jnp.broadcast_to(total, shape)
        return [
            jnp.sum(jnp.where(lane == kinds * row + kind, total, 0.0), axis=1, keepdims=True)
            for kind in range(kinds)
        ]

    def fold(a):
        return jnp.sum(a.reshape(days // 8, 8, a.shape[1]), axis=0)

    def folded(a, b):
        s = fold(a * b)
        return s[:, :TILE] + s[:, TILE:]

    def direction(k, s, at):
        return rs[at, half[s]] if k == 0 else p[s, at]

    def residue(k, s, at):
        return (rs if k == 0 else r)[at, half[s]]

    for k in range(ITERS):
        last = k == ITERS - 1
        for g in range(GROUPS):
            group = of_group(g)
            j = k * GROUPS + g
            if k > 0:
                rr, pw, rw, ww = totals(j - GROUPS, 4)
                alpha = rr / pw
                beta = (rr + alpha * (alpha * ww - 2.0 * rw)) / rr
                for i in range(per):
                    field = of_field(g * per + i)
                    a, b = alpha[i : i + 1], beta[i : i + 1]
                    for s in range(2):
                        old = direction(k - 1, s, field)
                        if k == 1:
                            x[field, half[s]] = a * old
                        else:
                            x[field, half[s]] += a * old
                        res = residue(k - 1, s, field) - a * w[k - 1, s, field]
                        r[field, half[s]] = res
                        p[s, field] = res + b * old
            first, second = (split(direction(k, s, group)) for s in range(2))
            near = dot(first, FIRST_FIRST) + dot(second, SECOND_FIRST)
            far = dot(first, FIRST_SECOND) + dot(second, SECOND_SECOND)
            for i in range(per):
                field = of_field(g * per + i)
                for s, coupled in ((0, near), (1, far)):
                    v = direction(k, s, field)
                    w[k, s, field] = (
                        diag[:, half[s]] * v + 0.5 * temporal(v)
                        - coupled[i * days : (i + 1) * days]
                    )

            @pl.when(me > 0)
            def _():
                to_next(k, g).wait_recv()

            @pl.when(me < n - 1)
            def _():
                to_prev(k, g).wait_recv()

            if k == 0:
                for dst in (p_right, r_right):
                    dst[group] = h_right[k, group]
                for dst in (p_left, r_left):
                    dst[group] = h_left[k, group]
            else:
                for i in range(per):
                    field = of_field(g * per + i)
                    a, b = alpha[i : i + 1], beta[i : i + 1]
                    for pp, res, new in ((p_left, r_left, h_left), (p_right, r_right, h_right)):
                        value = res[field] - a * new[k, field]
                        res[field] = value
                        pp[field] = value + b * pp[field]
            w[k, 0, group] -= p_left[group]
            w[k, 1, group] -= dot(split(p_right[group]), RIGHT_SECOND)
            if not last:
                cs[k + 1, group] = dot(split(w[k, 1, group]), SECOND_NEXT)

            parts = []
            for i in range(per):
                field = of_field(g * per + i)
                sums = [0.0] * (2 if last else 4)
                for s in range(2):
                    image, res = w[k, s, field], residue(k, s, field)
                    sums[0] += folded(res, res)
                    sums[1] += folded(direction(k, s, field), image)
                    if not last:
                        sums[2] += folded(res, image)
                        sums[3] += folded(image, image)
                parts.append(sums)
            send_sums(j, parts)
            if not last:
                @pl.when(me > 0)
                def _():
                    to_prev(k + 1, g).start()

                @pl.when(me < n - 1)
                def _():
                    to_next(k + 1, g).start()

    for g in range(GROUPS):
        rr, pw = totals((ITERS - 1) * GROUPS + g, 2)
        alpha = rr / pw
        for i in range(per):
            field = of_field(g * per + i)
            a = alpha[i : i + 1]
            for s in range(2):
                x[field, half[s]] += a * p[s, field]
                r[field, half[s]] -= a * w[ITERS - 1, s, field]

    for k in range(ITERS):
        for g in range(GROUPS):
            @pl.when(me > 0)
            def _():
                to_prev(k, g).wait_send()

            @pl.when(me < n - 1)
            def _():
                to_next(k, g).wait_send()

            sums_sent(k * GROUPS + g).wait()


def on_device(n, right_side, obs_prec, outlier_flags, up_one, up_two):
    nf, days, cells = right_side.shape
    rows = nf * days
    vmem = pl.BlockSpec(memory_space=pltpu.VMEM)
    side = pltpu.VMEM((rows, PAIR), F32)
    sides = pltpu.VMEM((ITERS, rows, PAIR), F32)
    dma = pltpu.SemaphoreType.DMA
    smoothed, residual = pl.pallas_call(
        functools.partial(kernel, n, nf, days),
        out_shape=[jax.ShapeDtypeStruct((rows, cells), F32)] * 2,
        in_specs=[pl.BlockSpec(memory_space=pltpu.HBM)] * 5,
        out_specs=[vmem] * 2,
        scratch_shapes=[
            pltpu.VMEM((rows, cells), F32),
            pltpu.VMEM(obs_prec.shape, F32),
            pltpu.VMEM(outlier_flags.shape, jnp.int32),
            pltpu.VMEM(up_one.shape, F32),
            pltpu.VMEM(up_two.shape, F32),
            pltpu.VMEM((6, PAIR, PAIR), BF16),
            pltpu.VMEM((6, PAIR, PAIR), BF16),
            pltpu.VMEM((days, cells), F32),
            pltpu.VMEM((2, rows, PAIR), F32),
            pltpu.VMEM((ITERS, 2, rows, PAIR), F32),
            sides, sides, sides,
            side, side, side, side,
            pltpu.VMEM((ITERS * GROUPS, n, 1, TILE), F32),
            dma((ITERS, GROUPS)), dma((ITERS, GROUPS)),
            dma((ITERS, GROUPS)), dma((ITERS, GROUPS)),
            dma((ITERS * GROUPS,)), dma((ITERS * GROUPS,)), dma((5,)),
        ],
        compiler_params=pltpu.CompilerParams(
            collective_id=0, has_side_effects=True, vmem_limit_bytes=63 * 2**20
        ),
        cost_estimate=pl.CostEstimate(
            flops=36 * ITERS * rows * PAIR * PAIR, bytes_accessed=12 * rows * cells, transcendentals=0
        ),
    )(right_side.reshape(rows, cells), obs_prec, outlier_flags, up_one, up_two)
    shape = (nf, days, cells)
    return smoothed.reshape(shape), residual.reshape(shape)


def solution(mesh):
    placed = (
        P("region", None, "space"),
        P("region", "space"),
        P("region", "space"),
        P("space", "region", None),
        P("space", "region", None),
    )
    return jax.shard_map(
        functools.partial(on_device, mesh.shape["space"]),
        mesh=mesh,
        in_specs=placed,
        out_specs=(P("region", None, "space"), P("region", None, "space")),
        check_vma=False,
    )
```
